32 devices in a mesh: lat: 4 (over x, core), lon: 8 (over z, y).
Axes of the slice: x: 2, y: 2, z: 4, core: 2. Of those that a mesh axis runs over, the one named last changes fastest.
Arguments:
- fields: bfloat16 [512, 1440, 256], P('lat', 'lon'), may hold values from -6 to 6
- basis: float32 [512, 4, 3, 17], P('lat'), may hold values from -1 to 1
- reach: int32 [512], P('lat'), may hold values from 1 to 8, as said below
- mixing: bfloat16 [4, 256, 256], replicated, may hold values from -0.1875 to 0.1875
- gains: float32 [2, 720, 256], replicated, may hold values from -5 to 5
Outputs:
- updated: bfloat16 [512, 1440, 256], P('lat', 'lon')
The draws below stay inside these ranges and needn't reach their ends.
Inputs may be any that keep to these rules, and one draw needn't show every extreme that they name: `reach`: 8 is reached in some row.
All inputs are finite; a program needn't handle non-finite values.
Results may differ from the reference program's by a relative error of at most 0.0062.
Values may be sent and summed in bfloat16 or wider, within the bound.
A program may use at most 576 MiB of HBM per device.

```python
import jax
import jax.numpy as jnp
from jax import lax

NLON = 1440
C = 256
MODES = 720
K = 4
HALO = 8
WIN = 17
LAT = 512


def draw_reach(key, part):
    first, second = jax.random.split(jax.random.fold_in(key, 11))
    values = jax.random.randint(first, (LAT,), 1, HALO + 1)
    where = jax.random.randint(second, (), 0, LAT)
    return values.at[where].set(HALO).astype(jnp.int32)


def block_scale(rng, shape, shards, low, largest):
    loudness, own = 1.0, jax.random.fold_in(rng, 6)
    for axis_at, parts in shards:
        draws = jnp.exp(jax.random.uniform(jax.random.fold_in(own, axis_at), (parts,), jnp.float32, low / len(shards), largest / len(shards)))
        loudness = loudness * jnp.repeat(draws, shape[axis_at] // parts).reshape([-1 if axis == axis_at else 1 for axis in range(len(shape))])
    return loudness


def bell_draw(key, extent, deviation, most, cuts=(), kind=jnp.bfloat16):
    array = deviation * jax.random.normal(key, extent, jnp.float32)
    if cuts:
        array = array * block_scale(key, extent, cuts, -0.22, 0.18)
    return jnp.clip(array, -most, most).astype(kind)


def setup_inputs(seed: int = 0) -> dict:
    arg_keys = jax.random.split(jax.random.key(seed), 6)
    return {
        "fields": bell_draw(arg_keys[0], (LAT, NLON, C), 1.0, 6.0, ((0, 4), (1, 8))),
        "basis": bell_draw(arg_keys[1], (LAT, K, 3, WIN), 0.15, 1.0, ((0, 4),), jnp.float32),
        "reach": draw_reach(jax.random.fold_in(arg_keys[5], 71), 0),
        "mixing": bell_draw(arg_keys[3], (K, C, C), (K * C) ** -0.5, 0.1875),
        "gains": bell_draw(arg_keys[4], (2, MODES, C), 1.0, 5.0, (), jnp.float32),
    }


def make_tables(count, modes):
    index = jnp.arange(count, dtype=jnp.int32)
    wave = jnp.arange(modes, dtype=jnp.int32)
    phase = (index[:, None] * wave[None, :]) % count
    angle = phase.astype(jnp.float32) * (2.0 * jnp.pi / count)
    cosine = jnp.cos(angle)
    sine = jnp.sin(angle)
    forward = jnp.concatenate([cosine, -sine], 1)
    weights = jnp.where(wave == 0, 1.0, 2.0).astype(jnp.float32) / count
    weights = jnp.concatenate([weights, weights], 0)
    adjoint = forward * weights[None, :]
    return forward.astype(jnp.bfloat16), adjoint.astype(jnp.bfloat16)


def reference(fields, basis, reach, mixing, gains):
    rows_all = fields.shape[0]
    wide = jnp.concatenate([fields[:, -HALO:], fields, fields[:, :HALO]], 1)
    zero_row = jnp.zeros((1,) + wide.shape[1:], jnp.bfloat16)
    padded = jnp.concatenate([zero_row, wide, zero_row], 0)
    offsets = jnp.arange(WIN, dtype=jnp.int32) - HALO
    mask = (jnp.abs(offsets)[None, :] <= reach[:, None]).astype(jnp.float32)
    filters = (basis * mask[:, None, None, :]).astype(jnp.bfloat16)
    forward, adjoint = make_tables(NLON, MODES)
    mix32 = mixing.astype(jnp.float32)

    def one_row(i):
        window = lax.dynamic_slice_in_dim(padded, i, 3, 0)
        filt = lax.dynamic_index_in_dim(filters, i, 0, keepdims=False).astype(jnp.float32)
        total = jnp.zeros((K, NLON, C), jnp.float32)
        for a in range(3):
            for b in range(WIN):
                total = total + filt[:, a, b][:, None, None] * window[a, b:b + NLON].astype(jnp.float32)[None]
        conv = total.astype(jnp.bfloat16).astype(jnp.float32)
        local = jnp.einsum('kjc,kcd->jd', conv, mix32)
        row = lax.dynamic_index_in_dim(fields, i, 0, keepdims=False)
        spectrum = jnp.dot(forward.T, row, preferred_element_type=jnp.float32)
        real = spectrum[:MODES]
        imag = spectrum[MODES:]
        filtered = jnp.concatenate([gains[0] * real - gains[1] * imag, gains[0] * imag + gains[1] * real], 0).astype(jnp.bfloat16)
        back = jnp.dot(adjoint, filtered, preferred_element_type=jnp.float32).astype(jnp.bfloat16)
        return (row.astype(jnp.float32) + local + back.astype(jnp.float32)).astype(jnp.bfloat16)

    return lax.map(one_row, jnp.arange(rows_all, dtype=jnp.int32))
```

```python
import functools

import jax
import jax.numpy as jnp
from jax import lax
from jax.experimental import pallas as pl
from jax.experimental.pallas import tpu as pltpu
from jax.sharding import PartitionSpec as P

NLON = 1440
MODES = 720
HALO = 8
WIN = 17
TILE = 64
SPAN = TILE + 2 * HALO
GROUP = 4
PARTS = 2
LIMIT = 48 * 1024 * 1024


def exchange(block, axis, dim, width, periodic):
    count = lax.axis_size(axis)
    forward = [(i, i + 1) for i in range(count - 1)]
    if periodic:
        forward.append((count - 1, 0))
    backward = [(target, source) for source, target in forward]
    low = lax.ppermute(
        lax.slice_in_dim(block, block.shape[dim] - width, None, axis=dim), axis, forward
    )
    high = lax.ppermute(lax.slice_in_dim(block, 0, width, axis=dim), axis, backward)
    return low, high


def tables(count, cols):
    wave = jnp.arange(MODES, dtype=jnp.int32)

    def phases(index):
        phase = index * wave % NLON
        return phase.astype(jnp.float32) * (2.0 * jnp.pi / NLON)

    index = jnp.arange(NLON, dtype=jnp.int32)
    angle = phases(index[:, None])
    forward = jnp.concatenate([jnp.cos(angle), -jnp.sin(angle)], 1)
    weights = jnp.where(wave == 0, 1.0, 2.0).astype(jnp.float32) / NLON
    weights = jnp.concatenate([weights, weights], 0)
    adjoint = (forward * weights[None, :]).astype(jnp.bfloat16)
    forward = forward.astype(jnp.bfloat16).reshape(count, cols, 2 * MODES)
    rows = -(-cols // 8) * 8
    adjoint = jnp.pad(adjoint.reshape(count, cols, 2 * MODES), ((0, 0), (0, rows - cols), (0, 0)))
    return forward.transpose(0, 2, 1), adjoint.reshape(count * rows, 2 * MODES)


def transform_kernel(count, cols, rows, x_ref, f_ref, a_ref, g_ref, o_ref, filtered):
    step = 240
    for at in range(0, MODES, step):
        real = jnp.zeros((step, x_ref.shape[-1]), jnp.float32)
        imag = real
        for s in range(count):
            x = x_ref[s, 0]
            real += jnp.dot(f_ref[s, at : at + step], x, preferred_element_type=jnp.float32)
            imag += jnp.dot(
                f_ref[s, MODES + at : MODES + at + step], x, preferred_element_type=jnp.float32
            )
        gain_real = g_ref[0, at : at + step]
        gain_imag = g_ref[1, at : at + step]
        filtered[at : at + step] = (gain_real * real - gain_imag * imag).astype(jnp.bfloat16)
        filtered[MODES + at : MODES + at + step] = (gain_real * imag + gain_imag * real).astype(
            jnp.bfloat16
        )
    back = jnp.dot(a_ref[...], filtered[...], preferred_element_type=jnp.float32)
    for s in range(count):
        o_ref[s, 0] = back[s * rows : s * rows + cols].astype(jnp.bfloat16)


def transform(piece, forward, adjoint, gains):
    count, height, cols, chans = piece.shape
    rows = -(-cols // 8) * 8
    block = pl.BlockSpec((count, 1, cols, chans), lambda r: (0, r, 0, 0))
    return pl.pallas_call(
        functools.partial(transform_kernel, count, cols, rows),
        grid=(height,),
        in_specs=[
            block,
            pl.BlockSpec(forward.shape, lambda r: (0, 0, 0)),
            pl.BlockSpec(adjoint.shape, lambda r: (0, 0)),
            pl.BlockSpec(gains.shape, lambda r: (0, 0, 0)),
        ],
        out_specs=block,
        out_shape=jax.ShapeDtypeStruct(piece.shape, jnp.bfloat16),
        scratch_shapes=[pltpu.VMEM((2 * MODES, chans), jnp.bfloat16)],
        compiler_params=pltpu.CompilerParams(vmem_limit_bytes=LIMIT),
        cost_estimate=pl.CostEstimate(
            flops=height * 4 * 2 * MODES * NLON * chans,
            bytes_accessed=4 * piece.size + 12_000_000,
            transcendentals=0,
        ),
        name="transform",
    )(piece, forward, adjoint, gains)


def local_kernel(tiles, w_ref, n0_ref, n1_ref, taps_ref, mix_ref, x_ref, o_ref, conv):
    basis_count = taps_ref.shape[1]
    chans = x_ref.shape[-1]
    cols = x_ref.shape[1]
    height = tiles * TILE
    zeros = jnp.zeros((256 - 3 * SPAN, chans), jnp.bfloat16)
    for r in range(GROUP):
        bands = []
        for k in range(basis_count):
            row = jnp.broadcast_to(taps_ref[r, k : k + 1], (TILE, 256))
            bands.append(pltpu.roll(row, 0, 1, stride=1, stride_axis=0).astype(jnp.bfloat16))
        band = jnp.concatenate(bands, 0)
        for t in range(tiles):
            at = slice(t * TILE, t * TILE + SPAN)
            pieces = []
            for a in range(3):
                if r + a < GROUP:
                    pieces.append(w_ref[r + a, at])
                elif r + a == GROUP:
                    pieces.append(n0_ref[0, at])
                else:
                    pieces.append(n1_ref[0, at])
            window = jnp.concatenate(pieces + [zeros], 0)
            out = jnp.dot(band, window, preferred_element_type=jnp.float32).astype(jnp.bfloat16)
            at = r * height + t * TILE
            for k in range(basis_count):
                conv[k, at : at + TILE] = out[k * TILE : (k + 1) * TILE]
    total = jnp.dot(conv[0], mix_ref[0], preferred_element_type=jnp.float32)
    for k in range(1, basis_count):
        total += jnp.dot(conv[k], mix_ref[k], preferred_element_type=jnp.float32)
    for r in range(GROUP):
        mixed = total[r * height : r * height + cols]
        o_ref[r] = (x_ref[r].astype(jnp.float32) + mixed).astype(jnp.bfloat16)


def local_part(fields, padded, taps, mixing):
    lat_rows, cols, chans = fields.shape
    wide = padded.shape[1]
    tiles = (wide - 2 * HALO) // TILE
    basis_count = mixing.shape[0]
    block = pl.BlockSpec((GROUP, cols, chans), lambda g: (g, 0, 0))
    return pl.pallas_call(
        functools.partial(local_kernel, tiles),
        grid=(lat_rows // GROUP,),
        in_specs=[
            pl.BlockSpec((GROUP, wide, chans), lambda g: (g, 0, 0)),
            pl.BlockSpec((1, wide, chans), lambda g: (g * GROUP + GROUP, 0, 0)),
            pl.BlockSpec((1, wide, chans), lambda g: (g * GROUP + GROUP + 1, 0, 0)),
            pl.BlockSpec((GROUP, basis_count, 256), lambda g: (g, 0, 0)),
            pl.BlockSpec(mixing.shape, lambda g: (0, 0, 0)),
            block,
        ],
        out_specs=block,
        out_shape=jax.ShapeDtypeStruct(fields.shape, jnp.bfloat16),
        scratch_shapes=[pltpu.VMEM((basis_count, GROUP * tiles * TILE, chans), jnp.bfloat16)],
        compiler_params=pltpu.CompilerParams(vmem_limit_bytes=LIMIT),
        cost_estimate=pl.CostEstimate(
            flops=2 * lat_rows * tiles * (256 * 256 * chans + TILE * basis_count * chans * chans),
            bytes_accessed=8 * padded.size,
            transcendentals=0,
        ),
        name="local",
    )(padded, padded, padded, taps, mixing, fields)


def add_kernel(base_ref, back_ref, o_ref):
    o_ref[...] = (base_ref[...].astype(jnp.float32) + back_ref[...].astype(jnp.float32)).astype(
        jnp.bfloat16
    )


def add_part(base, back, part):
    count, height, cols, chans = back.shape
    return pl.pallas_call(
        add_kernel,
        grid=(count,),
        in_specs=[
            pl.BlockSpec((1, height, cols, chans), lambda s: (s, part, 0, 0)),
            pl.BlockSpec((1, height, cols, chans), lambda s: (s, 0, 0, 0)),
        ],
        out_specs=pl.BlockSpec((1, height, cols, chans), lambda s: (s, part, 0, 0)),
        out_shape=jax.ShapeDtypeStruct(base.shape, jnp.bfloat16),
        input_output_aliases={0: 0},
        compiler_params=pltpu.CompilerParams(vmem_limit_bytes=LIMIT),
        cost_estimate=pl.CostEstimate(
            flops=back.size, bytes_accessed=6 * back.size, transcendentals=0
        ),
        name="add",
    )(base, back)


def shards(fields, basis, reach, mixing, gains):
    lat_rows, cols, chans = fields.shape
    count = lax.axis_size("lon")
    rows = lat_rows // count
    low, high = exchange(fields, "lon", 1, HALO, True)
    sent, low, high = lax.optimization_barrier((fields, low, high))
    split = sent.reshape(count, PARTS, rows // PARTS, cols, chans)
    gathered = [
        lax.all_to_all(split[:, q], "lon", split_axis=0, concat_axis=0, tiled=True)
        for q in range(PARTS)
    ]
    tiles = -(-cols // TILE)
    spare = jnp.zeros((lat_rows, tiles * TILE - cols, chans), jnp.bfloat16)
    wide = jnp.concatenate([low, fields, high, spare], 1)
    above, below = exchange(wide, "lat", 0, 1, False)
    padded = jnp.concatenate([above, wide, below], 0)
    offsets = jnp.arange(WIN, dtype=jnp.int32) - HALO
    mask = (jnp.abs(offsets)[None, :] <= reach[:, None]).astype(jnp.float32)
    filters = (basis * mask[:, None, None, :]).astype(jnp.bfloat16).astype(jnp.float32)
    taps = jnp.pad(filters, ((0, 0), (0, 0), (0, 0), (0, SPAN - WIN)))
    taps = jnp.pad(
        taps.reshape(lat_rows, basis.shape[1], 3 * SPAN), ((0, 0), (0, 0), (0, 256 - 3 * SPAN))
    )
    base = local_part(fields, padded, taps, mixing)
    forward, adjoint = tables(count, cols)
    first, base = lax.optimization_barrier((gathered[0], base))
    gathered = [first] + gathered[1:]
    backs = [
        lax.all_to_all(
            transform(piece, forward, adjoint, gains), "lon", split_axis=0, concat_axis=0, tiled=True
        )
        for piece in gathered
    ]
    total = base.reshape(count, rows, cols, chans)
    for part, back in enumerate(backs):
        total = add_part(total, back, part)
    return total.reshape(lat_rows, cols, chans)


def solution(mesh):
    return jax.shard_map(
        shards,
        mesh=mesh,
        in_specs=(P("lat", "lon", None), P("lat", None, None, None), P("lat"), P(), P()),
        out_specs=P("lat", "lon", None),
        check_vma=False,
    )
```

```python
import functools

import jax
import jax.numpy as jnp
from jax import lax
from jax.experimental import pallas as pl
from jax.experimental.pallas import tpu as pltpu
from jax.sharding import PartitionSpec as P

NLON = 1440
MODES = 720
HALO = 8
WIN = 17
TILE = 64
SPAN = TILE + 2 * HALO
GROUP = 4
PARTS = 2
LIMIT = 48 * 1024 * 1024


def exchange(block, axis, dim, width, periodic):
    count = lax.axis_size(axis)
    forward = [(i, i + 1) for i in range(count - 1)]
    if periodic:
        forward.append((count - 1, 0))
    backward = [(target, source) for source, target in forward]
    low = lax.ppermute(
        lax.slice_in_dim(block, block.shape[dim] - width, None, axis=dim), axis, forward
    )
    high = lax.ppermute(lax.slice_in_dim(block, 0, width, axis=dim), axis, backward)
    return low, high


def tables(count, cols):
    wave = jnp.arange(MODES, dtype=jnp.int32)

    def phases(index):
        phase = index * wave % NLON
        return phase.astype(jnp.float32) * (2.0 * jnp.pi / NLON)

    index = jnp.arange(NLON, dtype=jnp.int32)
    angle = phases(index[:, None])
    forward = jnp.concatenate([jnp.cos(angle), -jnp.sin(angle)], 1)
    weights = jnp.where(wave == 0, 1.0, 2.0).astype(jnp.float32) / NLON
    weights = jnp.concatenate([weights, weights], 0)
    adjoint = (forward * weights[None, :]).astype(jnp.bfloat16)
    forward = forward.astype(jnp.bfloat16).reshape(count, cols, 2 * MODES)
    rows = -(-cols // 8) * 8
    adjoint = jnp.pad(adjoint.reshape(count, cols, 2 * MODES), ((0, 0), (0, rows - cols), (0, 0)))
    return forward.transpose(0, 2, 1), adjoint.reshape(count * rows, 2 * MODES)


def transform_kernel(count, cols, rows, x_ref, f_ref, a_ref, g_ref, o_ref, filtered):
    step = 240
    for at in range(0, MODES, step):
        real = jnp.zeros((step, x_ref.shape[-1]), jnp.float32)
        imag = real
        for s in range(count):
            x = x_ref[s, 0]
            real += jnp.dot(f_ref[s, at : at + step], x, preferred_element_type=jnp.float32)
            imag += jnp.dot(
                f_ref[s, MODES + at : MODES + at + step], x, preferred_element_type=jnp.float32
            )
        gain_real = g_ref[0, at : at + step]
        gain_imag = g_ref[1, at : at + step]
        filtered[at : at + step] = (gain_real * real - gain_imag * imag).astype(jnp.bfloat16)
        filtered[MODES + at : MODES + at + step] = (gain_real * imag + gain_imag * real).astype(
            jnp.bfloat16
        )
    back = jnp.dot(a_ref[...], filtered[...], preferred_element_type=jnp.float32)
    for s in range(count):
        o_ref[s, 0] = back[s * rows : s * rows + cols].astype(jnp.bfloat16)


def transform(piece, forward, adjoint, gains):
    count, height, cols, chans = piece.shape
    rows = -(-cols // 8) * 8
    block = pl.BlockSpec((count, 1, cols, chans), lambda r: (0, r, 0, 0))
    return pl.pallas_call(
        functools.partial(transform_kernel, count, cols, rows),
        grid=(height,),
        in_specs=[
            block,
            pl.BlockSpec(forward.shape, lambda r: (0, 0, 0)),
            pl.BlockSpec(adjoint.shape, lambda r: (0, 0)),
            pl.BlockSpec(gains.shape, lambda r: (0, 0, 0)),
        ],
        out_specs=block,
        out_shape=jax.ShapeDtypeStruct(piece.shape, jnp.bfloat16),
        scratch_shapes=[pltpu.VMEM((2 * MODES, chans), jnp.bfloat16)],
        compiler_params=pltpu.CompilerParams(vmem_limit_bytes=LIMIT),
        cost_estimate=pl.CostEstimate(
            flops=height * 4 * 2 * MODES * NLON * chans,
            bytes_accessed=4 * piece.size + 12_000_000,
            transcendentals=0,
        ),
        name="transform",
    )(piece, forward, adjoint, gains)


def local_kernel(tiles, w_ref, n0_ref, n1_ref, taps_ref, mix_ref, x_ref, o_ref, conv):
    basis_count = taps_ref.shape[1]
    chans = x_ref.shape[-1]
    cols = x_ref.shape[1]
    height = tiles * TILE
    zeros = jnp.zeros((256 - 3 * SPAN, chans), jnp.bfloat16)
    for r in range(GROUP):
        bands = []
        for k in range(basis_count):
            row = jnp.broadcast_to(taps_ref[r, k : k + 1], (TILE, 256))
            bands.append(pltpu.roll(row, 0, 1, stride=1, stride_axis=0).astype(jnp.bfloat16))
        band = jnp.concatenate(bands, 0)
        for t in range(tiles):
            at = slice(t * TILE, t * TILE + SPAN)
            pieces = []
            for a in range(3):
                if r + a < GROUP:
                    pieces.append(w_ref[r + a, at])
                elif r + a == GROUP:
                    pieces.append(n0_ref[0, at])
                else:
                    pieces.append(n1_ref[0, at])
            window = jnp.concatenate(pieces + [zeros], 0)
            out = jnp.dot(band, window, preferred_element_type=jnp.float32).astype(jnp.bfloat16)
            at = r * height + t * TILE
            for k in range(basis_count):
                conv[k, at : at + TILE] = out[k * TILE : (k + 1) * TILE]
    total = jnp.dot(conv[0], mix_ref[0], preferred_element_type=jnp.float32)
    for k in range(1, basis_count):
        total += jnp.dot(conv[k], mix_ref[k], preferred_element_type=jnp.float32)
    for r in range(GROUP):
        mixed = total[r * height : r * height + cols]
        o_ref[r] = (x_ref[r].astype(jnp.float32) + mixed).astype(jnp.bfloat16)


def local_part(fields, padded, taps, mixing):
    lat_rows, cols, chans = fields.shape
    wide = padded.shape[1]
    tiles = (wide - 2 * HALO) // TILE
    basis_count = mixing.shape[0]
    block = pl.BlockSpec((GROUP, cols, chans), lambda g: (g, 0, 0))
    return pl.pallas_call(
        functools.partial(local_kernel, tiles),
        grid=(lat_rows // GROUP,),
        in_specs=[
            pl.BlockSpec((GROUP, wide, chans), lambda g: (g, 0, 0)),
            pl.BlockSpec((1, wide, chans), lambda g: (g * GROUP + GROUP, 0, 0)),
            pl.BlockSpec((1, wide, chans), lambda g: (g * GROUP + GROUP + 1, 0, 0)),
            pl.BlockSpec((GROUP, basis_count, 256), lambda g: (g, 0, 0)),
            pl.BlockSpec(mixing.shape, lambda g: (0, 0, 0)),
            block,
        ],
        out_specs=block,
        out_shape=jax.ShapeDtypeStruct(fields.shape, jnp.bfloat16),
        scratch_shapes=[pltpu.VMEM((basis_count, GROUP * tiles * TILE, chans), jnp.bfloat16)],
        compiler_params=pltpu.CompilerParams(vmem_limit_bytes=LIMIT),
        cost_estimate=pl.CostEstimate(
            flops=2 * lat_rows * tiles * (256 * 256 * chans + TILE * basis_count * chans * chans),
            bytes_accessed=8 * padded.size,
            transcendentals=0,
        ),
        name="local",
    )(padded, padded, padded, taps, mixing, fields)


def add_kernel(base_ref, back_ref, o_ref):
    for s in range(back_ref.shape[0]):
        o_ref[:, s, 0] = (
            base_ref[:, s, 0].astype(jnp.float32) + back_ref[s].astype(jnp.float32)
        ).astype(jnp.bfloat16)


def add_part(base, back, part):
    count, cols, height, chans = back.shape
    steps = 9 if cols % 9 == 0 else 1
    wide = pl.BlockSpec((cols // steps, count, 1, height, chans), lambda j: (j, 0, part, 0, 0))
    return pl.pallas_call(
        add_kernel,
        grid=(steps,),
        in_specs=[
            wide,
            pl.BlockSpec((count, cols // steps, height, chans), lambda j: (0, j, 0, 0)),
        ],
        out_specs=wide,
        out_shape=jax.ShapeDtypeStruct(base.shape, jnp.bfloat16),
        input_output_aliases={0: 0},
        compiler_params=pltpu.CompilerParams(vmem_limit_bytes=LIMIT),
        cost_estimate=pl.CostEstimate(
            flops=back.size, bytes_accessed=6 * back.size, transcendentals=0
        ),
        name="add",
    )(base, back)


def shards(fields, basis, reach, mixing, gains):
    lat_rows, cols, chans = fields.shape
    count = lax.axis_size("lon")
    rows = lat_rows // count
    split = fields.reshape(count, PARTS, rows // PARTS, cols, chans)

    def swap(piece):
        return lax.all_to_all(piece, "lon", split_axis=0, concat_axis=0, tiled=True)

    gathered = [swap(split[:, q]) for q in range(PARTS)]
    first, forward, adjoint = lax.optimization_barrier((gathered[0], *tables(count, cols)))
    results = [transform(piece, forward, adjoint, gains) for piece in [first] + gathered[1:]]
    near, _ = lax.optimization_barrier((fields, first))
    low, high = exchange(near, "lon", 1, HALO, True)
    ready, low, high = lax.optimization_barrier((results[0], low, high))
    backs = [swap(ready)]
    tiles = -(-cols // TILE)
    spare = jnp.zeros((lat_rows, tiles * TILE - cols, chans), jnp.bfloat16)
    wide = jnp.concatenate([low, fields, high, spare], 1)
    above, below = exchange(wide, "lat", 0, 1, False)
    padded = jnp.concatenate([above, wide, below], 0)
    offsets = jnp.arange(WIN, dtype=jnp.int32) - HALO
    mask = (jnp.abs(offsets)[None, :] <= reach[:, None]).astype(jnp.float32)
    filters = (basis * mask[:, None, None, :]).astype(jnp.bfloat16).astype(jnp.float32)
    taps = jnp.pad(filters, ((0, 0), (0, 0), (0, 0), (0, SPAN - WIN)))
    taps = jnp.pad(
        taps.reshape(lat_rows, basis.shape[1], 3 * SPAN), ((0, 0), (0, 0), (0, 256 - 3 * SPAN))
    )
    base = local_part(fields, padded, taps, mixing)
    *ready, base = lax.optimization_barrier((*results[1:], base))
    backs += [swap(result) for result in ready]
    total = base.transpose(1, 0, 2).reshape(cols, count, PARTS, rows // PARTS, chans)
    for part, back in enumerate(backs):
        total = add_part(total, back.transpose(0, 2, 1, 3), part)
    return total.reshape(cols, lat_rows, chans).transpose(1, 0, 2)


def solution(mesh):
    return jax.shard_map(
        shards,
        mesh=mesh,
        in_specs=(P("lat", "lon", None), P("lat", None, None, None), P("lat"), P(), P()),
        out_specs=P("lat", "lon", None),
        check_vma=False,
    )
```

```python
import functools

import jax
import jax.numpy as jnp
from jax import lax
from jax.experimental import pallas as pl
from jax.experimental.pallas import tpu as pltpu
from jax.sharding import PartitionSpec as P

NLON = 1440
MODES = 720
HALO = 8
WIN = 17
TILE = 64
SPAN = TILE + 2 * HALO
GROUP = 4
PARTS = 2
LIMIT = 48 * 1024 * 1024


def exchange(block, axis, dim, width, periodic):
    count = lax.axis_size(axis)
    forward = [(i, i + 1) for i in range(count - 1)]
    if periodic:
        forward.append((count - 1, 0))
    backward = [(target, source) for source, target in forward]
    low = lax.ppermute(
        lax.slice_in_dim(block, block.shape[dim] - width, None, axis=dim), axis, forward
    )
    high = lax.ppermute(lax.slice_in_dim(block, 0, width, axis=dim), axis, backward)
    return low, high


def tables(count, cols):
    wave = jnp.arange(MODES, dtype=jnp.int32)

    def phases(index):
        phase = index * wave % NLON
        return phase.astype(jnp.float32) * (2.0 * jnp.pi / NLON)

    index = jnp.arange(NLON, dtype=jnp.int32)
    angle = phases(index[:, None])
    forward = jnp.concatenate([jnp.cos(angle), -jnp.sin(angle)], 1)
    weights = jnp.where(wave == 0, 1.0, 2.0).astype(jnp.float32) / NLON
    weights = jnp.concatenate([weights, weights], 0)
    adjoint = (forward * weights[None, :]).astype(jnp.bfloat16)
    forward = forward.astype(jnp.bfloat16).reshape(count, cols, 2 * MODES)
    rows = -(-cols // 8) * 8
    adjoint = jnp.pad(adjoint.reshape(count, cols, 2 * MODES), ((0, 0), (0, rows - cols), (0, 0)))
    return forward.transpose(0, 2, 1), adjoint.reshape(count * rows, 2 * MODES)


def transform_kernel(count, cols, rows, x_ref, f_ref, a_ref, g_ref, o_ref, filtered):
    step = 240
    for at in range(0, MODES, step):
        real = jnp.zeros((step, x_ref.shape[-1]), jnp.float32)
        imag = real
        for s in range(count):
            x = x_ref[s, 0]
            real += jnp.dot(f_ref[s, at : at + step], x, preferred_element_type=jnp.float32)
            imag += jnp.dot(
                f_ref[s, MODES + at : MODES + at + step], x, preferred_element_type=jnp.float32
            )
        gain_real = g_ref[0, at : at + step]
        gain_imag = g_ref[1, at : at + step]
        filtered[at : at + step] = (gain_real * real - gain_imag * imag).astype(jnp.bfloat16)
        filtered[MODES + at : MODES + at + step] = (gain_real * imag + gain_imag * real).astype(
            jnp.bfloat16
        )
    back = jnp.dot(a_ref[...], filtered[...], preferred_element_type=jnp.float32)
    for s in range(count):
        o_ref[s, 0] = back[s * rows : s * rows + cols].astype(jnp.bfloat16)


def transform(piece, forward, adjoint, gains):
    count, height, cols, chans = piece.shape
    rows = -(-cols // 8) * 8
    block = pl.BlockSpec((count, 1, cols, chans), lambda r: (0, r, 0, 0))
    return pl.pallas_call(
        functools.partial(transform_kernel, count, cols, rows),
        grid=(height,),
        in_specs=[
            block,
            pl.BlockSpec(forward.shape, lambda r: (0, 0, 0)),
            pl.BlockSpec(adjoint.shape, lambda r: (0, 0)),
            pl.BlockSpec(gains.shape, lambda r: (0, 0, 0)),
        ],
        out_specs=block,
        out_shape=jax.ShapeDtypeStruct(piece.shape, jnp.bfloat16),
        scratch_shapes=[pltpu.VMEM((2 * MODES, chans), jnp.bfloat16)],
        compiler_params=pltpu.CompilerParams(vmem_limit_bytes=LIMIT),
        cost_estimate=pl.CostEstimate(
            flops=height * 4 * 2 * MODES * NLON * chans,
            bytes_accessed=4 * piece.size + 12_000_000,
            transcendentals=0,
        ),
        name="transform",
    )(piece, forward, adjoint, gains)


def local_kernel(tiles, w_ref, n0_ref, n1_ref, taps_ref, mix_ref, x_ref, o_ref, conv):
    basis_count = taps_ref.shape[1]
    chans = x_ref.shape[-1]
    cols = x_ref.shape[1]
    height = tiles * TILE
    zeros = jnp.zeros((256 - 3 * SPAN, chans), jnp.bfloat16)
    for r in range(GROUP):
        bands = []
        for k in range(basis_count):
            row = jnp.broadcast_to(taps_ref[r, k : k + 1], (TILE, 256))
            bands.append(pltpu.roll(row, 0, 1, stride=1, stride_axis=0).astype(jnp.bfloat16))
        band = jnp.concatenate(bands, 0)
        for t in range(tiles):
            at = slice(t * TILE, t * TILE + SPAN)
            pieces = []
            for a in range(3):
                if r + a < GROUP:
                    pieces.append(w_ref[r + a, at])
                elif r + a == GROUP:
                    pieces.append(n0_ref[0, at])
                else:
                    pieces.append(n1_ref[0, at])
            window = jnp.concatenate(pieces + [zeros], 0)
            out = jnp.dot(band, window, preferred_element_type=jnp.float32).astype(jnp.bfloat16)
            at = r * height + t * TILE
            for k in range(basis_count):
                conv[k, at : at + TILE] = out[k * TILE : (k + 1) * TILE]
    total = jnp.dot(conv[0], mix_ref[0], preferred_element_type=jnp.float32)
    for k in range(1, basis_count):
        total += jnp.dot(conv[k], mix_ref[k], preferred_element_type=jnp.float32)
    for r in range(GROUP):
        mixed = total[r * height : r * height + cols]
        o_ref[r] = (x_ref[r].astype(jnp.float32) + mixed).astype(jnp.bfloat16)


def local_part(fields, padded, taps, mixing):
    lat_rows, cols, chans = fields.shape
    wide = padded.shape[1]
    tiles = (wide - 2 * HALO) // TILE
    basis_count = mixing.shape[0]
    block = pl.BlockSpec((GROUP, cols, chans), lambda g: (g, 0, 0))
    return pl.pallas_call(
        functools.partial(local_kernel, tiles),
        grid=(lat_rows // GROUP,),
        in_specs=[
            pl.BlockSpec((GROUP, wide, chans), lambda g: (g, 0, 0)),
            pl.BlockSpec((1, wide, chans), lambda g: (g * GROUP + GROUP, 0, 0)),
            pl.BlockSpec((1, wide, chans), lambda g: (g * GROUP + GROUP + 1, 0, 0)),
            pl.BlockSpec((GROUP, basis_count, 256), lambda g: (g, 0, 0)),
            pl.BlockSpec(mixing.shape, lambda g: (0, 0, 0)),
            block,
        ],
        out_specs=block,
        out_shape=jax.ShapeDtypeStruct(fields.shape, jnp.bfloat16),
        scratch_shapes=[pltpu.VMEM((basis_count, GROUP * tiles * TILE, chans), jnp.bfloat16)],
        compiler_params=pltpu.CompilerParams(vmem_limit_bytes=LIMIT),
        cost_estimate=pl.CostEstimate(
            flops=2 * lat_rows * tiles * (256 * 256 * chans + TILE * basis_count * chans * chans),
            bytes_accessed=8 * padded.size,
            transcendentals=0,
        ),
        name="local",
    )(padded, padded, padded, taps, mixing, fields)


def add_kernel(base_ref, back_ref, o_ref):
    for s in range(back_ref.shape[0]):
        o_ref[:, s, 0] = (
            base_ref[:, s, 0].astype(jnp.float32) + back_ref[s].astype(jnp.float32)
        ).astype(jnp.bfloat16)


def add_part(base, back, part):
    count, cols, height, chans = back.shape
    steps = 9 if cols % 9 == 0 else 1
    wide = pl.BlockSpec((cols // steps, count, 1, height, chans), lambda j: (j, 0, part, 0, 0))
    return pl.pallas_call(
        add_kernel,
        grid=(steps,),
        in_specs=[
            wide,
            pl.BlockSpec((count, cols // steps, height, chans), lambda j: (0, j, 0, 0)),
        ],
        out_specs=wide,
        out_shape=jax.ShapeDtypeStruct(base.shape, jnp.bfloat16),
        input_output_aliases={0: 0},
        compiler_params=pltpu.CompilerParams(vmem_limit_bytes=LIMIT),
        cost_estimate=pl.CostEstimate(
            flops=back.size, bytes_accessed=6 * back.size, transcendentals=0
        ),
        name="add",
    )(base, back)


def shards(fields, basis, reach, mixing, gains):
    lat_rows, cols, chans = fields.shape
    count = lax.axis_size("lon")
    rows = lat_rows // count
    split = fields.reshape(count, PARTS, rows // PARTS, cols, chans)

    def swap(piece):
        return lax.all_to_all(piece, "lon", split_axis=0, concat_axis=0, tiled=True)

    head, split = lax.optimization_barrier((split[:, 0], split))
    gathered = [swap(head)] + [swap(split[:, q]) for q in range(1, PARTS)]
    first, forward, adjoint = lax.optimization_barrier((gathered[0], *tables(count, cols)))
    results = [transform(piece, forward, adjoint, gains) for piece in [first] + gathered[1:]]
    near, _ = lax.optimization_barrier((fields, first))
    low, high = exchange(near, "lon", 1, HALO, True)
    ready, low, high = lax.optimization_barrier((results[0], low, high))
    backs = [swap(ready)]
    tiles = -(-cols // TILE)
    spare = jnp.zeros((lat_rows, tiles * TILE - cols, chans), jnp.bfloat16)
    wide = jnp.concatenate([low, fields, high, spare], 1)
    above, below = exchange(wide, "lat", 0, 1, False)
    padded = jnp.concatenate([above, wide, below], 0)
    offsets = jnp.arange(WIN, dtype=jnp.int32) - HALO
    mask = (jnp.abs(offsets)[None, :] <= reach[:, None]).astype(jnp.float32)
    filters = (basis * mask[:, None, None, :]).astype(jnp.bfloat16).astype(jnp.float32)
    taps = jnp.pad(filters, ((0, 0), (0, 0), (0, 0), (0, SPAN - WIN)))
    taps = jnp.pad(
        taps.reshape(lat_rows, basis.shape[1], 3 * SPAN), ((0, 0), (0, 0), (0, 256 - 3 * SPAN))
    )
    base = local_part(fields, padded, taps, mixing)
    *ready, base = lax.optimization_barrier((*results[1:], base))
    backs += [swap(result) for result in ready]
    total = base.transpose(1, 0, 2).reshape(cols, count, PARTS, rows // PARTS, chans)
    for part, back in enumerate(backs):
        total = add_part(total, back.transpose(0, 2, 1, 3), part)
    return total.reshape(cols, lat_rows, chans).transpose(1, 0, 2)


def solution(mesh):
    return jax.shard_map(
        shards,
        mesh=mesh,
        in_specs=(P("lat", "lon", None), P("lat", None, None, None), P("lat"), P(), P()),
        out_specs=P("lat", "lon", None),
        check_vma=False,
    )
```
